32 devices in a mesh: seq: 4 (over y, x), tile: 8 (over z, core).
Axes of the slice: x: 2, y: 2, z: 4, core: 2. Of those that a mesh axis runs over, the one named last changes fastest.
Arguments:
- states: int32 [512, 384], P('seq'), may hold values from 0 to 20
- tile_blocks: int32 [8, 2], P('tile'), may hold values from 0 to 3, as said below
- couplings: bfloat16 [8, 2016, 2016], P('tile'), may hold values from -0.875 to 0.875
- fields: float32 [8064], P('tile'), may hold values from -8 to 305
Outputs:
- probs: bfloat16 [512, 8064], P('seq', 'tile')
- grad_couplings: float32 [8, 2016, 2016], P('tile', 'seq')
The draws below stay inside these ranges and needn't reach their ends.
Inputs may be any that keep to these rules, and one draw needn't show every extreme that they name: `tile_blocks`: every tile names two blocks; each block is named by exactly three tiles: one naming it twice and two that pair it with another block; no unordered pair of blocks is named by two tiles.
All inputs are finite; a program needn't handle non-finite values.
Results may differ from the reference program's by a relative error of at most 0.023.
Values may be sent and summed in bfloat16 or wider, within the bound.
A program may use at most 128 MiB of HBM per device.

```python
import math
import jax
import jax.numpy as jnp
import numpy as np
from jax import lax

Q = 21
LB = 96
B_DEV = 128
NB = 4
L = 384
LQ = 2016
SEQS = 512
N_SEQ = 4
N_TILE = 8


def draw_tile_blocks(key, part):
    key = jax.random.fold_in(key, 5)
    order_key, place_key = jax.random.split(key)
    order = jax.random.permutation(order_key, NB).astype(jnp.int32)
    following = jnp.roll(order, -1)
    cycle_pairs = jnp.stack([order, following], axis=1)
    self_pairs = jnp.stack([order, order], axis=1)
    pairs = jnp.concatenate([cycle_pairs, self_pairs], axis=0)
    placement_order = jax.random.permutation(place_key, 2 * NB)
    return pairs[placement_order].astype(jnp.int32)


def draw_fields(key, part):
    key = jax.random.fold_in(key, 11)
    keys = jax.random.split(key, 1)
    values = jnp.clip(1.5 * jax.random.normal(keys[0], (L, Q), jnp.float32), -8.0, 8.0)
    return values.reshape(L * Q)


def plant(values, key, low, top_value):
    longest = values.shape.index(max(values.shape))
    spots = []
    for shift in (0, 1):
        where = [jax.random.randint(jax.random.fold_in(key, axis), (), 0, length) for axis, length in enumerate(values.shape)]
        where[longest] = (where[longest] + shift) % values.shape[longest]
        spots.append(tuple(where))
    return values.at[spots[0]].set(low).at[spots[1]].set(top_value)


def steps_of(own_key, shape, cuts, low, high):
    level, own = 1.0, jax.random.fold_in(own_key, 6)
    for position, blocks in cuts:
        steps = jnp.exp(jax.random.uniform(jax.random.fold_in(own, position), (blocks,), jnp.float32, low / len(cuts), high / len(cuts)))
        level = level * jnp.repeat(steps, shape[position] // blocks).reshape([-1 if axis == position else 1 for axis in range(len(shape))])
    return level


def rank_table(number_of, slope):
    weights = [(1 << 20) // math.isqrt(rank ** slope) + 1 for rank in range(1, number_of + 1)]
    spread = 1 + sum(weights) // (1 << 30)
    return np.cumsum(np.array([max(1, weight // spread) for weight in weights]))


def ranked(stream_key, shape, count, skew):
    grid = rank_table(count, skew)
    pick = jax.random.randint(jax.random.fold_in(stream_key, 1), shape, 0, int(grid[count - 1]))
    rank = jnp.searchsorted(jnp.asarray(grid, jnp.int32), pick, side="right")
    return jax.random.permutation(jax.random.fold_in(stream_key, 2), count)[rank].astype(jnp.int32)


def bell_draw(own_key, shape, spread, most, cuts=(), kind=jnp.bfloat16):
    array = spread * jax.random.normal(own_key, shape, jnp.float32)
    if cuts:
        array = array * steps_of(own_key, shape, cuts, -0.22, 0.18)
    return jnp.clip(array, -most, most).astype(kind)


def setup_inputs(seed: int = 0) -> dict:
    arg_keys = jax.random.split(jax.random.key(seed), 5)
    states = plant(ranked(arg_keys[0], (SEQS, L), Q, 2), jax.random.fold_in(arg_keys[0], 3), 0, Q - 1).astype(jnp.int32)
    tile_blocks = draw_tile_blocks(jax.random.fold_in(arg_keys[4], 71), 0)
    couplings = bell_draw(arg_keys[2], (N_TILE, LQ, LQ), (3.0 / (4 * LB) ** 0.5), 0.875, ((0, 8),))
    fields = draw_fields(jax.random.fold_in(arg_keys[4], 71), 0)
    return {"states": states, "tile_blocks": tile_blocks, "couplings": couplings, "fields": fields}


def state_table(block_states):
    state_codes = jnp.arange(Q, dtype=jnp.int32)
    matches = block_states[:, :, None] == state_codes[None, None, :]
    return matches.astype(jnp.float32).reshape(block_states.shape[0], LB * Q)

def self_mask(lead_block, tail_block):
    residue = jnp.arange(LB * Q, dtype=jnp.int32) // Q
    keep_mask = jnp.logical_or(lead_block != tail_block, residue[:, None] != residue[None, :])
    return keep_mask.astype(jnp.float32)

def rounded(values):
    return lax.optimization_barrier(values.astype(jnp.bfloat16)).astype(jnp.float32)

def pull_rows(weights, block_states):

    def add_residue(running, residue_index):
        chosen_rows = lax.dynamic_slice_in_dim(weights, residue_index * Q, Q, 0)
        codes_here = lax.dynamic_index_in_dim(block_states, residue_index, 1, False)
        return (running + jnp.take(chosen_rows, codes_here, axis=0), None)
    start_value = jnp.zeros((block_states.shape[0], weights.shape[1]), jnp.float32)
    running, unused = lax.scan(add_residue, start_value, jnp.arange(LB, dtype=jnp.int32))
    return running

def count_rows(values, block_states):
    row_total = values.shape[0]
    group_codes = jnp.arange(row_total, dtype=jnp.int32) // B_DEV * Q

    def one_residue(residue_index):
        codes_here = lax.dynamic_index_in_dim(block_states, residue_index, 1, False)
        return jax.ops.segment_sum(values, group_codes + codes_here, num_segments=N_SEQ * Q)
    stacked = lax.map(one_residue, jnp.arange(LB, dtype=jnp.int32))
    stacked = stacked.reshape(LB, N_SEQ, Q, values.shape[1])
    return jnp.transpose(stacked, (1, 0, 2, 3)).reshape(N_SEQ, LB * Q, values.shape[1])

def reference(states, tile_blocks, couplings, fields):
    row_total = states.shape[0]
    block_width = LB * Q

    def add_tile(field_total, tile_item):
        tile_pair, weights = tile_item
        lead_block = tile_pair[0]
        tail_block = tile_pair[1]
        masked = weights.astype(jnp.float32) * self_mask(lead_block, tail_block)
        lead_states = lax.dynamic_slice_in_dim(states, lead_block * LB, LB, 1)
        tail_states = lax.dynamic_slice_in_dim(states, tail_block * LB, LB, 1)
        to_lead = pull_rows(masked.T, tail_states)
        to_tail = pull_rows(masked, lead_states)
        same_block = lead_block == tail_block
        lead_part = rounded(jnp.where(same_block, to_lead + to_tail, to_lead))
        tail_part = rounded(jnp.where(same_block, jnp.zeros_like(to_tail), to_tail))
        lead_start = lead_block * block_width
        tail_start = tail_block * block_width
        current = lax.dynamic_slice_in_dim(field_total, lead_start, block_width, 1)
        field_total = lax.dynamic_update_slice_in_dim(field_total, current + lead_part, lead_start, 1)
        current = lax.dynamic_slice_in_dim(field_total, tail_start, block_width, 1)
        field_total = lax.dynamic_update_slice_in_dim(field_total, current + tail_part, tail_start, 1)
        return (field_total, None)
    start_total = jnp.zeros((row_total, L * Q), jnp.float32)
    field_total, unused = lax.scan(add_tile, start_total, (tile_blocks, couplings))
    logits = field_total.reshape(row_total, L, Q) + fields.reshape(L, Q)[None, :, :]
    row_max = lax.optimization_barrier(jnp.max(logits, axis=2, keepdims=True))
    exponent = jnp.exp(logits - row_max)
    probs = (exponent / lax.optimization_barrier(jnp.sum(exponent, axis=2, keepdims=True))).astype(jnp.bfloat16).reshape(row_total, L * Q)
    grad_scale = Q / math.sqrt(row_total)

    def tile_grad(tile_pair):
        lead_block = tile_pair[0]
        tail_block = tile_pair[1]
        lead_states = lax.dynamic_slice_in_dim(states, lead_block * LB, LB, 1)
        tail_states = lax.dynamic_slice_in_dim(states, tail_block * LB, LB, 1)
        lead_probs = lax.dynamic_slice_in_dim(probs, lead_block * block_width, block_width, 1).astype(jnp.float32)
        tail_probs = lax.dynamic_slice_in_dim(probs, tail_block * block_width, block_width, 1).astype(jnp.float32)
        lead_gap = rounded(lead_probs - state_table(lead_states))
        tail_gap = rounded(tail_probs - state_table(tail_states))
        grad_term = jnp.transpose(count_rows(lead_gap, tail_states), (0, 2, 1)) + count_rows(tail_gap, lead_states)
        partials = rounded(grad_term * self_mask(lead_block, tail_block)[None, :, :] * grad_scale)
        return lax.optimization_barrier(jnp.sum(partials, axis=0))
    grads = lax.map(tile_grad, tile_blocks)
    return (probs, grads)
```

```python
import functools
import math

import jax
import jax.numpy as jnp
from jax import lax
from jax.experimental import pallas as pl
from jax.experimental.pallas import tpu as pltpu
from jax.sharding import PartitionSpec as P

Q = 21
LB = 96
WIDTH = LB * Q
HALF = WIDTH // 2
CHUNKS = 4


def state_table(block_states):
    state_codes = jnp.arange(Q, dtype=jnp.int32)
    matches = block_states[:, :, None] == state_codes[None, None, :]
    return matches.astype(jnp.bfloat16).reshape(block_states.shape[0], block_states.shape[1] * Q)


def normalize(logits):
    row_total = logits.shape[0]
    shaped = logits.reshape(row_total, -1, Q)
    row_max = jnp.max(shaped, axis=2, keepdims=True)
    exponent = jnp.exp(shaped - row_max)
    result = exponent / jnp.sum(exponent, axis=2, keepdims=True)
    return result.astype(jnp.bfloat16).reshape(row_total, -1)


def send(src, dst, send_sem, recv_sem, **device):
    return pltpu.make_async_remote_copy(
        src_ref=src,
        dst_ref=dst,
        send_sem=send_sem,
        recv_sem=recv_sem,
        device_id=device,
        device_id_type=pl.DeviceIdType.MESH,
    )


def greet(groups, seqs):
    tile = lax.axis_index("tile")
    group, core = tile // 2, tile % 2
    seq = lax.axis_index("seq")
    barrier = pltpu.get_barrier_semaphore()
    mesh_id = pl.DeviceIdType.MESH
    pl.semaphore_signal(
        barrier, inc=1, device_id={"tile": group * 2 + 1 - core}, device_id_type=mesh_id
    )
    for k in range(1, groups):
        pl.semaphore_signal(
            barrier,
            inc=1,
            device_id={"tile": ((group + k) % groups) * 2 + core},
            device_id_type=mesh_id,
        )
    for k in range(1, seqs):
        pl.semaphore_signal(
            barrier, inc=1, device_id={"seq": (seq + k) % seqs}, device_id_type=mesh_id
        )
    pl.semaphore_wait(barrier, groups + max(seqs - 1, 0))


def reduce_kernel(
    groups, blocks, lead, tail, out, halves, mine, stage, mate_in, onward, arrived, sems
):
    tile = lax.axis_index("tile")
    group, core = tile // 2, tile % 2
    mate = group * 2 + 1 - core
    lead_block, tail_block = blocks[0, 0], blocks[0, 1]
    for h in range(2):
        halves[0, h] = lead[:, h * HALF : (h + 1) * HALF]
        halves[1, h] = tail[:, h * HALF : (h + 1) * HALF]

    def part(g, h):
        in_lead = (lead_block == g).astype(jnp.float32)
        in_tail = (tail_block == g).astype(jnp.float32)
        return (halves[0, h] * in_lead + halves[1, h] * in_tail).astype(jnp.bfloat16)

    greet(groups, 0)

    def to_mate(k):
        return send(stage.at[k], mate_in.at[k], sems.at[0, k], sems.at[1, k], tile=mate)

    def to_owner(k):
        owner = ((group + k) % groups) * 2 + core
        return send(onward.at[k], arrived.at[k], sems.at[2, k], sems.at[3, k], tile=owner)

    def first(k, carry):
        k = (k + 1) % groups
        stage[k] = part((group + k) % groups, 1 - core)
        to_mate(k).start()
        return carry

    lax.fori_loop(0, groups, first, 0)

    def second(k, carry):
        mine[...] = part((group + k) % groups, core).astype(jnp.float32)
        to_mate(k).wait_recv()
        onward[k] = (mine[...] + mate_in[k].astype(jnp.float32)).astype(jnp.bfloat16)
        to_owner(k).start()
        return carry

    lax.fori_loop(1, groups, second, 0)
    to_mate(0).wait_recv()
    mine[...] = part(group, core).astype(jnp.float32) + mate_in[0].astype(jnp.float32)

    def third(k, carry):
        to_owner(k).wait()
        mine[...] += arrived[k].astype(jnp.float32)
        return carry

    lax.fori_loop(1, groups, third, 0)

    def fourth(k, carry):
        to_mate(k).wait_send()
        return carry

    lax.fori_loop(0, groups, fourth, 0)
    out[...] = mine[...]


def exchange_kernel(groups, seqs, blocks, probs, tails, leads, *scratch):
    every = scratch[:CHUNKS]
    tail_out = scratch[CHUNKS : 2 * CHUNKS]
    lead_out, near, pair, over = scratch[2 * CHUNKS :]
    tile = lax.axis_index("tile")
    group, core = tile // 2, tile % 2
    seq = lax.axis_index("seq")
    mate = group * 2 + 1 - core
    lead_block, tail_block = blocks[0, 0], blocks[0, 1]
    rows = probs.shape[0] // CHUNKS
    share = WIDTH // seqs
    greet(groups, seqs)

    def to_group(c, k):
        other = ((group + k) % groups) * 2 + core
        mine = every[c].at[group, core]
        return send(mine, mine, near.at[0, c, k], near.at[1, c, k], tile=other)

    def to_mate(c, k):
        block = every[c].at[(group + groups - k) % groups, core]
        return send(block, block, pair.at[0, c, k], pair.at[1, c, k], tile=mate)

    def tail_to(c, k):
        place = tails.at[seq, pl.ds(c * rows, rows)]
        return send(tail_out[c], place, over.at[0, c, k], over.at[1, c, k], seq=(seq + k) % seqs)

    def lead_to(c, k):
        other = (seq + k) % seqs
        place = leads.at[seq, pl.ds(c * rows, rows)]
        return send(
            lead_out.at[c, other], place, over.at[2, c, k], over.at[3, c, k], seq=other
        )

    for c in range(CHUNKS):
        every[c][group, core] = probs[c * rows : (c + 1) * rows]

        def start_far(k, carry, c=c):
            to_group(c, k).start()
            return carry

        lax.fori_loop(1, groups, start_far, 0)
        to_mate(c, 0).start()

    for c in range(CHUNKS):

        def relay(k, carry, c=c):
            to_group(c, k).wait_recv()
            to_mate(c, k).start()
            return carry

        lax.fori_loop(1, groups, relay, 0)

        def gathered(k, carry, c=c):
            to_mate(c, k).wait_recv()
            return carry

        lax.fori_loop(0, groups, gathered, 0)
        for h in range(2):
            tail_out[c][:, h * HALF : (h + 1) * HALF] = every[c][tail_block, h]
            block_half = every[c][lead_block, h]
            for j in range(seqs // 2):
                lead_out[c, h * (seqs // 2) + j] = block_half[:, j * share : (j + 1) * share]

        def start_over(k, carry, c=c):
            tail_to(c, k).start()
            lead_to(c, k).start()
            return carry

        lax.fori_loop(1, seqs, start_over, 0)
        tails[seq, c * rows : (c + 1) * rows] = tail_out[c][...]
        leads[seq, c * rows : (c + 1) * rows] = lead_out[c, seq]

    for c in range(CHUNKS):

        def finish(k, carry, c=c):
            tail_to(c, k).wait()
            lead_to(c, k).wait()
            return carry

        lax.fori_loop(1, seqs, finish, 0)

        def sent_far(k, carry, c=c):
            to_group(c, k).wait_send()
            return carry

        lax.fori_loop(1, groups, sent_far, 0)

        def sent_pair(k, carry, c=c):
            to_mate(c, k).wait_send()
            return carry

        lax.fori_loop(0, groups, sent_pair, 0)


def reduce_fields(tile_blocks, lead, tail, groups):
    rows = lead.shape[0]
    slots = pltpu.VMEM((groups, rows, HALF), jnp.bfloat16)
    vmem = pl.BlockSpec(memory_space=pltpu.VMEM)
    return pl.pallas_call(
        functools.partial(reduce_kernel, groups),
        out_shape=jax.ShapeDtypeStruct((rows, HALF), jnp.float32),
        in_specs=[pl.BlockSpec(memory_space=pltpu.SMEM), vmem, vmem],
        out_specs=vmem,
        scratch_shapes=[
            pltpu.VMEM((2, 2, rows, HALF), jnp.float32),
            pltpu.VMEM((rows, HALF), jnp.float32),
            slots,
            slots,
            slots,
            slots,
            pltpu.SemaphoreType.DMA((4, groups)),
        ],
        compiler_params=pltpu.CompilerParams(
            collective_id=0, has_side_effects=True, vmem_limit_bytes=48 << 20
        ),
    )(tile_blocks, lead, tail)


def exchange(tile_blocks, probs, groups, seqs):
    rows = probs.shape[0]
    part = rows // CHUNKS
    vmem = pl.BlockSpec(memory_space=pltpu.VMEM)
    return pl.pallas_call(
        functools.partial(exchange_kernel, groups, seqs),
        out_shape=[
            jax.ShapeDtypeStruct((seqs, rows, WIDTH), jnp.bfloat16),
            jax.ShapeDtypeStruct((seqs, rows, WIDTH // seqs), jnp.bfloat16),
        ],
        in_specs=[pl.BlockSpec(memory_space=pltpu.SMEM), vmem],
        out_specs=[vmem, vmem],
        scratch_shapes=[pltpu.VMEM((groups, 2, part, HALF), jnp.bfloat16)] * CHUNKS
        + [pltpu.VMEM((part, WIDTH), jnp.bfloat16)] * CHUNKS
        + [
            pltpu.VMEM((CHUNKS, seqs, part, WIDTH // seqs), jnp.bfloat16),
            pltpu.SemaphoreType.DMA((2, CHUNKS, groups)),
            pltpu.SemaphoreType.DMA((2, CHUNKS, groups)),
            pltpu.SemaphoreType.DMA((4, CHUNKS, seqs)),
        ],
        compiler_params=pltpu.CompilerParams(
            collective_id=1, has_side_effects=True, vmem_limit_bytes=48 << 20
        ),
    )(tile_blocks, probs)


def body(states, tile_blocks, couplings, fields):
    groups = lax.axis_size("tile") // 2
    seqs = lax.axis_size("seq")
    seq = lax.axis_index("seq")
    row_total = states.shape[0] * seqs
    share = WIDTH // seqs
    lead_block = tile_blocks[0, 0]
    tail_block = tile_blocks[0, 1]
    apart = lead_block != tail_block
    residue = jnp.arange(WIDTH, dtype=jnp.int32) // Q
    keep_mask = jnp.logical_or(apart, residue[:, None] != residue[None, :])
    masked = jnp.where(keep_mask, couplings[0], jnp.zeros((), jnp.bfloat16))
    lead_states = lax.dynamic_slice_in_dim(states, lead_block * LB, LB, 1)
    tail_states = lax.dynamic_slice_in_dim(states, tail_block * LB, LB, 1)
    both_states = lax.all_gather(
        jnp.concatenate([lead_states, tail_states], axis=1), "seq", axis=0, tiled=True
    )
    lead = lax.dot_general(
        state_table(tail_states),
        masked,
        (((1,), (1,)), ((), ())),
        preferred_element_type=jnp.float32,
    )
    tail = jnp.dot(state_table(lead_states), masked, preferred_element_type=jnp.float32)
    logits = reduce_fields(tile_blocks, lead, tail, groups)
    probs = normalize(logits + fields[None, :])
    tail_probs, lead_probs = exchange(tile_blocks, probs, groups, seqs)
    tail_probs = tail_probs.reshape(row_total, WIDTH)
    lead_probs = lead_probs.reshape(row_total, share)
    share_states = lax.dynamic_slice_in_dim(both_states, seq * (LB // seqs), LB // seqs, 1)
    lead_table = state_table(share_states)
    tail_table = state_table(both_states[:, LB:])
    lead_gap = lead_probs - lead_table
    tail_gap = tail_probs - tail_table
    grad = lax.dot_general(
        lead_gap, tail_table, (((0,), (0,)), ((), ())), preferred_element_type=jnp.float32
    )
    grad = grad + lax.dot_general(
        lead_table, tail_gap, (((0,), (0,)), ((), ())), preferred_element_type=jnp.float32
    )
    grad_scale = Q / math.sqrt(row_total)
    own_residue = seq * (LB // seqs) + jnp.arange(share, dtype=jnp.int32) // Q
    own_mask = jnp.logical_or(apart, own_residue[:, None] != residue[None, :])
    grad = jnp.where(own_mask, grad * grad_scale, jnp.zeros((), jnp.float32))
    return (probs, grad[None])


def solution(mesh):
    in_specs = (P("seq", None), P("tile", None), P("tile", None, None), P("tile"))
    out_specs = (P("seq", "tile"), P("tile", "seq", None))
    return jax.shard_map(body, mesh=mesh, in_specs=in_specs, out_specs=out_specs, check_vma=False)
```

```python
import functools
import math

import jax
import jax.numpy as jnp
from jax import lax
from jax.experimental import pallas as pl
from jax.experimental.pallas import tpu as pltpu
from jax.sharding import PartitionSpec as P

Q = 21
LB = 96
WIDTH = LB * Q
HALF = WIDTH // 2
CHUNKS = 4
ROW_TILE = WIDTH // 6
COLUMN_TILE = 512


def residue_of(index):
    return (index * 3121) >> 16


def table(states, first, columns):
    lanes = states.shape[1]
    residue = residue_of(lax.broadcasted_iota(jnp.int32, (lanes, columns), 1)) + first
    place = lax.broadcasted_iota(jnp.int32, (lanes, columns), 0) == residue
    spread = jnp.dot(
        states, place.astype(jnp.float32).astype(jnp.bfloat16), preferred_element_type=jnp.float32
    )
    column = lax.broadcasted_iota(jnp.int32, (1, columns), 1)
    code = (column - residue_of(column) * Q).astype(jnp.float32)
    return jnp.where(spread == code, 1.0, 0.0)


def normalize(logits):
    row_total = logits.shape[0]
    shaped = logits.reshape(row_total, -1, Q)
    row_max = jnp.max(shaped, axis=2, keepdims=True)
    exponent = jnp.exp(shaped - row_max)
    result = exponent / jnp.sum(exponent, axis=2, keepdims=True)
    return result.astype(jnp.bfloat16).reshape(row_total, -1)


def field_kernel(blocks, states, weights, lead, tail, tail_table):
    step = pl.program_id(0)
    rows, width = weights.shape[1], weights.shape[2]
    first = step * (rows // Q)

    @pl.when(step == 0)
    def _():
        tail_table[...] = table(states[:, 128:], 0, width).astype(jnp.bfloat16)
        tail[...] = jnp.zeros_like(tail)

    own = residue_of(lax.broadcasted_iota(jnp.int32, (rows, 1), 0)) + first
    own = jnp.where(blocks[0, 0] == blocks[0, 1], own, -1)
    other = residue_of(lax.broadcasted_iota(jnp.int32, (1, width), 1))
    kept = jnp.where(own == other, 0.0, weights[0].astype(jnp.float32)).astype(jnp.bfloat16)
    lead_table = table(states[:, :128], first, rows).astype(jnp.bfloat16)
    lead[0] = lax.dot_general(
        tail_table[...], kept, (((1,), (1,)), ((), ())), preferred_element_type=jnp.float32
    )
    tail[...] += jnp.dot(lead_table, kept, preferred_element_type=jnp.float32)


def tile_fields(tile_blocks, states, couplings):
    rows = states.shape[0]
    return pl.pallas_call(
        field_kernel,
        grid=(WIDTH // ROW_TILE,),
        out_shape=[
            jax.ShapeDtypeStruct((WIDTH // ROW_TILE, rows, ROW_TILE), jnp.float32),
            jax.ShapeDtypeStruct((rows, WIDTH), jnp.float32),
        ],
        in_specs=[
            pl.BlockSpec(memory_space=pltpu.SMEM),
            pl.BlockSpec((rows, 256), lambda i: (0, 0)),
            pl.BlockSpec((1, ROW_TILE, WIDTH), lambda i: (0, i, 0)),
        ],
        out_specs=[
            pl.BlockSpec((1, rows, ROW_TILE), lambda i: (i, 0, 0)),
            pl.BlockSpec((rows, WIDTH), lambda i: (0, 0)),
        ],
        scratch_shapes=[pltpu.VMEM((rows, WIDTH), jnp.bfloat16)],
        compiler_params=pltpu.CompilerParams(vmem_limit_bytes=40 << 20),
    )(tile_blocks, states, couplings)


def gradient_kernel(blocks, states, lead_probs, tail_probs, grad, left):
    step = pl.program_id(0)
    rows, share = lead_probs.shape
    columns = tail_probs.shape[1]
    first = lax.axis_index("seq") * (share // Q)

    @pl.when(step == 0)
    def _():
        row = lax.broadcasted_iota(jnp.int32, (share, 128), 0)
        lane = lax.broadcasted_iota(jnp.int32, (share, 128), 1)
        place = (lane == residue_of(row) + first).astype(jnp.float32).astype(jnp.bfloat16)
        spread = lax.dot_general(
            place, states[:, :128], (((1,), (1,)), ((), ())), preferred_element_type=jnp.float32
        )
        row = lax.broadcasted_iota(jnp.int32, (share, 1), 0)
        code = (row - residue_of(row) * Q).astype(jnp.float32)
        lead_table = jnp.where(spread == code, 1.0, 0.0)
        lead_gap = lead_probs[...].astype(jnp.float32).T - lead_table
        left[:, :rows] = lead_gap.astype(jnp.bfloat16)
        left[:, rows:] = lead_table.astype(jnp.bfloat16)

    lanes = 128
    start = step * columns
    residue = residue_of(lax.broadcasted_iota(jnp.int32, (lanes, columns), 1) + start)
    place = lax.broadcasted_iota(jnp.int32, (lanes, columns), 0) == residue
    spread = jnp.dot(
        states[:, 128:],
        place.astype(jnp.float32).astype(jnp.bfloat16),
        preferred_element_type=jnp.float32,
    )
    column = lax.broadcasted_iota(jnp.int32, (1, columns), 1) + start
    other = residue_of(column)
    code = (column - other * Q).astype(jnp.float32)
    tail_table = jnp.where(spread == code, 1.0, 0.0)
    tail_gap = (tail_probs[...].astype(jnp.float32) - tail_table).astype(jnp.bfloat16)
    total = jnp.dot(
        left[:, :rows], tail_table.astype(jnp.bfloat16), preferred_element_type=jnp.float32
    )
    total = total + jnp.dot(left[:, rows:], tail_gap, preferred_element_type=jnp.float32)
    own = residue_of(lax.broadcasted_iota(jnp.int32, (share, 1), 0)) + first
    own = jnp.where(blocks[0, 0] == blocks[0, 1], own, -1)
    grad[...] = jnp.where(own == other, 0.0, total * (Q / math.sqrt(rows)))


def gradient(tile_blocks, states, lead_probs, tail_probs):
    rows, share = lead_probs.shape
    return pl.pallas_call(
        gradient_kernel,
        grid=(pl.cdiv(WIDTH, COLUMN_TILE),),
        out_shape=jax.ShapeDtypeStruct((share, WIDTH), jnp.float32),
        in_specs=[
            pl.BlockSpec(memory_space=pltpu.SMEM),
            pl.BlockSpec((rows, 256), lambda i: (0, 0)),
            pl.BlockSpec((rows, share), lambda i: (0, 0)),
            pl.BlockSpec((rows, COLUMN_TILE), lambda i: (0, i)),
        ],
        out_specs=pl.BlockSpec((share, COLUMN_TILE), lambda i: (0, i)),
        scratch_shapes=[pltpu.VMEM((share, 2 * rows), jnp.bfloat16)],
        compiler_params=pltpu.CompilerParams(vmem_limit_bytes=40 << 20),
    )(tile_blocks, states, lead_probs, tail_probs)


def send(src, dst, send_sem, recv_sem, **device):
    return pltpu.make_async_remote_copy(
        src_ref=src,
        dst_ref=dst,
        send_sem=send_sem,
        recv_sem=recv_sem,
        device_id=device,
        device_id_type=pl.DeviceIdType.MESH,
    )


def greet(groups, seqs):
    tile = lax.axis_index("tile")
    group, core = tile // 2, tile % 2
    seq = lax.axis_index("seq")
    barrier = pltpu.get_barrier_semaphore()
    mesh_id = pl.DeviceIdType.MESH
    pl.semaphore_signal(
        barrier, inc=1, device_id={"tile": group * 2 + 1 - core}, device_id_type=mesh_id
    )
    for k in range(1, groups):
        pl.semaphore_signal(
            barrier,
            inc=1,
            device_id={"tile": ((group + k) % groups) * 2 + core},
            device_id_type=mesh_id,
        )
    for k in range(1, seqs):
        pl.semaphore_signal(
            barrier, inc=1, device_id={"seq": (seq + k) % seqs}, device_id_type=mesh_id
        )
    pl.semaphore_wait(barrier, groups + max(seqs - 1, 0))


def reduce_kernel(
    groups,
    seqs,
    blocks,
    lead,
    tail,
    states,
    out,
    all_states,
    halves,
    mine,
    stage,
    mate_in,
    onward,
    arrived,
    sems,
    state_sems,
):
    tile = lax.axis_index("tile")
    group, core = tile // 2, tile % 2
    mate = group * 2 + 1 - core
    lead_block, tail_block = blocks[0, 0], blocks[0, 1]
    seq = lax.axis_index("seq")
    for h in range(2):
        for j in range(lead.shape[0] // 2):
            place = slice(j * ROW_TILE, (j + 1) * ROW_TILE)
            halves[0, h, :, place] = lead[h * (lead.shape[0] // 2) + j]
        halves[1, h] = tail[:, h * HALF : (h + 1) * HALF]

    def part(g, h):
        in_lead = (lead_block == g).astype(jnp.float32)
        in_tail = (tail_block == g).astype(jnp.float32)
        return (halves[0, h] * in_lead + halves[1, h] * in_tail).astype(jnp.bfloat16)

    greet(groups, seqs)

    def states_to(k):
        other = (seq + k) % seqs
        place = all_states.at[seq]
        return send(states, place, state_sems.at[0, k], state_sems.at[1, k], seq=other)

    def to_mate(k):
        return send(stage.at[k], mate_in.at[k], sems.at[0, k], sems.at[1, k], tile=mate)

    def to_owner(k):
        owner = ((group + k) % groups) * 2 + core
        return send(onward.at[k], arrived.at[k], sems.at[2, k], sems.at[3, k], tile=owner)

    def first(k, carry):
        k = (k + 1) % groups
        stage[k] = part((group + k) % groups, 1 - core)
        to_mate(k).start()
        return carry

    lax.fori_loop(0, groups, first, 0)

    def start_states(k, carry):
        states_to(k).start()
        return carry

    lax.fori_loop(1, seqs, start_states, 0)
    all_states[seq] = states[...]

    def second(k, carry):
        mine[...] = part((group + k) % groups, core).astype(jnp.float32)
        to_mate(k).wait_recv()
        onward[k] = (mine[...] + mate_in[k].astype(jnp.float32)).astype(jnp.bfloat16)
        to_owner(k).start()
        return carry

    lax.fori_loop(1, groups, second, 0)
    to_mate(0).wait_recv()
    mine[...] = part(group, core).astype(jnp.float32) + mate_in[0].astype(jnp.float32)

    def third(k, carry):
        to_owner(k).wait()
        mine[...] += arrived[k].astype(jnp.float32)
        return carry

    lax.fori_loop(1, groups, third, 0)

    def fourth(k, carry):
        to_mate(k).wait_send()
        return carry

    lax.fori_loop(0, groups, fourth, 0)

    def finish_states(k, carry):
        states_to(k).wait()
        return carry

    lax.fori_loop(1, seqs, finish_states, 0)
    out[...] = mine[...]


def exchange_kernel(groups, seqs, blocks, probs, tails, leads, *scratch):
    every = scratch[:CHUNKS]
    tail_out = scratch[CHUNKS : 2 * CHUNKS]
    lead_out, near, pair, over = scratch[2 * CHUNKS :]
    tile = lax.axis_index("tile")
    group, core = tile // 2, tile % 2
    seq = lax.axis_index("seq")
    mate = group * 2 + 1 - core
    lead_block, tail_block = blocks[0, 0], blocks[0, 1]
    rows = probs.shape[0] // CHUNKS
    share = WIDTH // seqs
    greet(groups, seqs)

    def to_group(c, k):
        other = ((group + k) % groups) * 2 + core
        mine = every[c].at[group, core]
        return send(mine, mine, near.at[0, c, k], near.at[1, c, k], tile=other)

    def to_mate(c, k):
        block = every[c].at[(group + groups - k) % groups, core]
        return send(block, block, pair.at[0, c, k], pair.at[1, c, k], tile=mate)

    def tail_to(c, k):
        place = tails.at[seq, pl.ds(c * rows, rows)]
        return send(tail_out[c], place, over.at[0, c, k], over.at[1, c, k], seq=(seq + k) % seqs)

    def lead_to(c, k):
        other = (seq + k) % seqs
        place = leads.at[seq, pl.ds(c * rows, rows)]
        return send(
            lead_out.at[c, other], place, over.at[2, c, k], over.at[3, c, k], seq=other
        )

    def begin(c):
        every[c][group, core] = probs[c * rows : (c + 1) * rows]

        def start_far(k, carry):
            to_group(c, k).start()
            return carry

        lax.fori_loop(1, groups, start_far, 0)
        to_mate(c, 0).start()

    begin(0)
    begin(1)

    for c in range(CHUNKS):

        def relay(k, carry, c=c):
            to_group(c, k).wait_recv()
            to_mate(c, k).start()
            return carry

        lax.fori_loop(1, groups, relay, 0)
        if c + 2 < CHUNKS:
            begin(c + 2)

        def gathered(k, carry, c=c):
            to_mate(c, k).wait_recv()
            return carry

        lax.fori_loop(0, groups, gathered, 0)
        for h in range(2):
            tail_out[c][:, h * HALF : (h + 1) * HALF] = every[c][tail_block, h]
            block_half = every[c][lead_block, h]
            for j in range(seqs // 2):
                lead_out[c, h * (seqs // 2) + j] = block_half[:, j * share : (j + 1) * share]

        def start_over(k, carry, c=c):
            tail_to(c, k).start()
            lead_to(c, k).start()
            return carry

        lax.fori_loop(1, seqs, start_over, 0)
        tails[seq, c * rows : (c + 1) * rows] = tail_out[c][...]
        leads[seq, c * rows : (c + 1) * rows] = lead_out[c, seq]

    for c in range(CHUNKS):

        def finish(k, carry, c=c):
            tail_to(c, k).wait()
            lead_to(c, k).wait()
            return carry

        lax.fori_loop(1, seqs, finish, 0)

        def sent_far(k, carry, c=c):
            to_group(c, k).wait_send()
            return carry

        lax.fori_loop(1, groups, sent_far, 0)

        def sent_pair(k, carry, c=c):
            to_mate(c, k).wait_send()
            return carry

        lax.fori_loop(0, groups, sent_pair, 0)


def reduce_fields(tile_blocks, lead, tail, states, groups, seqs):
    rows = tail.shape[0]
    slots = pltpu.VMEM((groups, rows, HALF), jnp.bfloat16)
    vmem = pl.BlockSpec(memory_space=pltpu.VMEM)
    return pl.pallas_call(
        functools.partial(reduce_kernel, groups, seqs),
        out_shape=[
            jax.ShapeDtypeStruct((rows, HALF), jnp.float32),
            jax.ShapeDtypeStruct((seqs,) + states.shape, jnp.bfloat16),
        ],
        in_specs=[pl.BlockSpec(memory_space=pltpu.SMEM), vmem, vmem, vmem],
        out_specs=[vmem, vmem],
        scratch_shapes=[
            pltpu.VMEM((2, 2, rows, HALF), jnp.float32),
            pltpu.VMEM((rows, HALF), jnp.float32),
            slots,
            slots,
            slots,
            slots,
            pltpu.SemaphoreType.DMA((4, groups)),
            pltpu.SemaphoreType.DMA((2, seqs)),
        ],
        compiler_params=pltpu.CompilerParams(
            collective_id=0, has_side_effects=True, vmem_limit_bytes=48 << 20
        ),
    )(tile_blocks, lead, tail, states)


def exchange(tile_blocks, probs, groups, seqs):
    rows = probs.shape[0]
    part = rows // CHUNKS
    vmem = pl.BlockSpec(memory_space=pltpu.VMEM)
    return pl.pallas_call(
        functools.partial(exchange_kernel, groups, seqs),
        out_shape=[
            jax.ShapeDtypeStruct((seqs, rows, WIDTH), jnp.bfloat16),
            jax.ShapeDtypeStruct((seqs, rows, WIDTH // seqs), jnp.bfloat16),
        ],
        in_specs=[pl.BlockSpec(memory_space=pltpu.SMEM), vmem],
        out_specs=[vmem, vmem],
        scratch_shapes=[pltpu.VMEM((groups, 2, part, HALF), jnp.bfloat16)] * CHUNKS
        + [pltpu.VMEM((part, WIDTH), jnp.bfloat16)] * CHUNKS
        + [
            pltpu.VMEM((CHUNKS, seqs, part, WIDTH // seqs), jnp.bfloat16),
            pltpu.SemaphoreType.DMA((2, CHUNKS, groups)),
            pltpu.SemaphoreType.DMA((2, CHUNKS, groups)),
            pltpu.SemaphoreType.DMA((4, CHUNKS, seqs)),
        ],
        compiler_params=pltpu.CompilerParams(
            collective_id=1, has_side_effects=True, vmem_limit_bytes=48 << 20
        ),
    )(tile_blocks, probs)


def body(states, tile_blocks, couplings, fields):
    groups = lax.axis_size("tile") // 2
    seqs = lax.axis_size("seq")
    row_total = states.shape[0] * seqs
    share = WIDTH // seqs
    picked = [
        jnp.pad(
            lax.dynamic_slice_in_dim(states, tile_blocks[0, side] * LB, LB, 1),
            ((0, 0), (0, 128 - LB)),
        )
        for side in range(2)
    ]
    own_states = jnp.concatenate(picked, axis=1).astype(jnp.bfloat16)
    lead, tail = tile_fields(tile_blocks, own_states, couplings)
    logits, all_states = reduce_fields(tile_blocks, lead, tail, own_states, groups, seqs)
    probs = normalize(logits + fields[None, :])
    tail_probs, lead_probs = exchange(tile_blocks, probs, groups, seqs)
    grad = gradient(
        tile_blocks,
        all_states.reshape(row_total, 256),
        lead_probs.reshape(row_total, share),
        tail_probs.reshape(row_total, WIDTH),
    )
    return (probs, grad[None])


def solution(mesh):
    in_specs = (P("seq", None), P("tile", None), P("tile", None, None), P("tile"))
    out_specs = (P("seq", "tile"), P("tile", "seq", None))
    return jax.shard_map(body, mesh=mesh, in_specs=in_specs, out_specs=out_specs, check_vma=False)
```

```python
import functools
import math

import jax
import jax.numpy as jnp
from jax import lax
from jax.experimental import pallas as pl
from jax.experimental.pallas import tpu as pltpu
from jax.sharding import PartitionSpec as P

Q = 21
LB = 96
WIDTH = LB * Q
HALF = WIDTH // 2
CHUNKS = 4
ROW_TILE = WIDTH // 6
COLUMN_TILE = 512


def residue_of(index):
    return (index * 3121) >> 16


def table(states, first, columns):
    lanes = states.shape[1]
    residue = residue_of(lax.broadcasted_iota(jnp.int32, (lanes, columns), 1)) + first
    place = lax.broadcasted_iota(jnp.int32, (lanes, columns), 0) == residue
    spread = jnp.dot(
        states, place.astype(jnp.float32).astype(jnp.bfloat16), preferred_element_type=jnp.float32
    )
    column = lax.broadcasted_iota(jnp.int32, (1, columns), 1)
    code = (column - residue_of(column) * Q).astype(jnp.float32)
    return jnp.where(spread == code, 1.0, 0.0)


def normalize(logits):
    lanes = logits.shape[1]
    lane = lax.broadcasted_iota(jnp.int32, (1, lanes), 1)
    place = lane - residue_of(lane) * Q
    shifts = (1, 2, 4, 8, 16)
    top = logits
    for shift in shifts:
        top = jnp.where(place >= shift, jnp.maximum(top, pltpu.roll(top, shift, 1)), top)
    for shift in shifts:
        back = pltpu.roll(top, lanes - shift, 1)
        top = jnp.where(place + shift < Q, jnp.maximum(top, back), top)
    exponent = jnp.exp(logits - top)
    total = exponent
    for shift in shifts:
        total = total + jnp.where(place >= shift, pltpu.roll(total, shift, 1), 0.0)
    total = jnp.where(place == Q - 1, total, 0.0)
    for shift in shifts:
        back = pltpu.roll(total, lanes - shift, 1)
        total = jnp.where(place + shift < Q, jnp.maximum(total, back), total)
    return exponent / total


def field_kernel(blocks, codes, weights, lead, tail, tail_table, states):
    step = pl.program_id(0)
    rows, width = weights.shape[1], weights.shape[2]
    first = step * (rows // Q)

    @pl.when(step == 0)
    def _():
        states[...] = codes[...].astype(jnp.float32).astype(jnp.bfloat16)
        tail_table[...] = table(states[...], blocks[0, 1] * LB, width).astype(jnp.bfloat16)
        tail[...] = jnp.zeros_like(tail)

    own = residue_of(lax.broadcasted_iota(jnp.int32, (rows, 1), 0)) + first
    own = jnp.where(blocks[0, 0] == blocks[0, 1], own, -1)
    other = residue_of(lax.broadcasted_iota(jnp.int32, (1, width), 1))
    kept = jnp.where(own == other, 0.0, weights[0].astype(jnp.float32)).astype(jnp.bfloat16)
    lead_table = table(states[...], blocks[0, 0] * LB + first, rows).astype(jnp.bfloat16)
    lead[0] = lax.dot_general(
        tail_table[...], kept, (((1,), (1,)), ((), ())), preferred_element_type=jnp.float32
    )
    tail[...] += jnp.dot(lead_table, kept, preferred_element_type=jnp.float32)


def tile_fields(tile_blocks, states, couplings):
    rows = states.shape[0]
    return pl.pallas_call(
        field_kernel,
        grid=(WIDTH // ROW_TILE,),
        out_shape=[
            jax.ShapeDtypeStruct((WIDTH // ROW_TILE, rows, ROW_TILE), jnp.float32),
            jax.ShapeDtypeStruct((rows, WIDTH), jnp.float32),
        ],
        in_specs=[
            pl.BlockSpec(memory_space=pltpu.SMEM),
            pl.BlockSpec(states.shape, lambda i: (0, 0)),
            pl.BlockSpec((1, ROW_TILE, WIDTH), lambda i: (0, i, 0)),
        ],
        out_specs=[
            pl.BlockSpec((1, rows, ROW_TILE), lambda i: (i, 0, 0)),
            pl.BlockSpec((rows, WIDTH), lambda i: (0, 0)),
        ],
        scratch_shapes=[
            pltpu.VMEM((rows, WIDTH), jnp.bfloat16),
            pltpu.VMEM(states.shape, jnp.bfloat16),
        ],
        compiler_params=pltpu.CompilerParams(vmem_limit_bytes=60 << 20),
    )(tile_blocks, states, couplings)


def gradient_kernel(blocks, states, lead_probs, tail_probs, grad, left):
    step = pl.program_id(0)
    rows, share = lead_probs.shape
    columns = tail_probs.shape[1]
    first = lax.axis_index("seq") * (share // Q)
    lanes = states.shape[1]

    @pl.when(step == 0)
    def _():
        row = lax.broadcasted_iota(jnp.int32, (share, lanes), 0)
        lane = lax.broadcasted_iota(jnp.int32, (share, lanes), 1)
        here = residue_of(row) + first + blocks[0, 0] * LB
        place = (lane == here).astype(jnp.float32).astype(jnp.bfloat16)
        spread = lax.dot_general(
            place, states[...], (((1,), (1,)), ((), ())), preferred_element_type=jnp.float32
        )
        row = lax.broadcasted_iota(jnp.int32, (share, 1), 0)
        code = (row - residue_of(row) * Q).astype(jnp.float32)
        lead_table = jnp.where(spread == code, 1.0, 0.0)
        lead_gap = lead_probs[...].astype(jnp.float32).T - lead_table
        left[:, :rows] = lead_gap.astype(jnp.bfloat16)
        left[:, rows:] = lead_table.astype(jnp.bfloat16)

    start = step * columns
    residue = residue_of(lax.broadcasted_iota(jnp.int32, (lanes, columns), 1) + start)
    here = residue + blocks[0, 1] * LB
    place = lax.broadcasted_iota(jnp.int32, (lanes, columns), 0) == here
    spread = jnp.dot(
        states[...],
        place.astype(jnp.float32).astype(jnp.bfloat16),
        preferred_element_type=jnp.float32,
    )
    column = lax.broadcasted_iota(jnp.int32, (1, columns), 1) + start
    other = residue_of(column)
    code = (column - other * Q).astype(jnp.float32)
    tail_table = jnp.where(spread == code, 1.0, 0.0)
    tail_gap = (tail_probs[...].astype(jnp.float32) - tail_table).astype(jnp.bfloat16)
    total = jnp.dot(
        left[:, :rows], tail_table.astype(jnp.bfloat16), preferred_element_type=jnp.float32
    )
    total = total + jnp.dot(left[:, rows:], tail_gap, preferred_element_type=jnp.float32)
    own = residue_of(lax.broadcasted_iota(jnp.int32, (share, 1), 0)) + first
    own = jnp.where(blocks[0, 0] == blocks[0, 1], own, -1)
    grad[...] = jnp.where(own == other, 0.0, total * (Q / math.sqrt(rows)))


def gradient(tile_blocks, states, lead_probs, tail_probs):
    rows, share = lead_probs.shape
    return pl.pallas_call(
        gradient_kernel,
        grid=(pl.cdiv(WIDTH, COLUMN_TILE),),
        out_shape=jax.ShapeDtypeStruct((share, WIDTH), jnp.float32),
        in_specs=[
            pl.BlockSpec(memory_space=pltpu.SMEM),
            pl.BlockSpec(states.shape, lambda i: (0, 0)),
            pl.BlockSpec((rows, share), lambda i: (0, 0)),
            pl.BlockSpec((rows, COLUMN_TILE), lambda i: (0, i)),
        ],
        out_specs=pl.BlockSpec((share, COLUMN_TILE), lambda i: (0, i)),
        scratch_shapes=[pltpu.VMEM((share, 2 * rows), jnp.bfloat16)],
        compiler_params=pltpu.CompilerParams(vmem_limit_bytes=40 << 20),
    )(tile_blocks, states, lead_probs, tail_probs)


def send(src, dst, send_sem, recv_sem, **device):
    return pltpu.make_async_remote_copy(
        src_ref=src,
        dst_ref=dst,
        send_sem=send_sem,
        recv_sem=recv_sem,
        device_id=device,
        device_id_type=pl.DeviceIdType.MESH,
    )


def greet(groups, seqs):
    tile = lax.axis_index("tile")
    group, core = tile // 2, tile % 2
    seq = lax.axis_index("seq")
    barrier = pltpu.get_barrier_semaphore()
    mesh_id = pl.DeviceIdType.MESH
    pl.semaphore_signal(
        barrier, inc=1, device_id={"tile": group * 2 + 1 - core}, device_id_type=mesh_id
    )
    for k in range(1, groups):
        pl.semaphore_signal(
            barrier,
            inc=1,
            device_id={"tile": ((group + k) % groups) * 2 + core},
            device_id_type=mesh_id,
        )
    for k in range(1, seqs):
        pl.semaphore_signal(
            barrier, inc=1, device_id={"seq": (seq + k) % seqs}, device_id_type=mesh_id
        )
    pl.semaphore_wait(barrier, groups + max(seqs - 1, 0))


def exchange_kernel(
    groups, seqs, blocks, lead, tail, codes, fields, probs, tails, leads, states, *scratch
):
    every = scratch[:CHUNKS]
    tail_out = scratch[CHUNKS : 2 * CHUNKS]
    (lead_out, halves, logits, stage, mate_in, onward, arrived) = scratch[2 * CHUNKS : -6]
    (halved, summed, near, pair, over, shared) = scratch[-6:]
    tile = lax.axis_index("tile")
    group, core = tile // 2, tile % 2
    seq = lax.axis_index("seq")
    mate = group * 2 + 1 - core
    lead_block, tail_block = blocks[0, 0], blocks[0, 1]
    rows = probs.shape[0] // CHUNKS
    share = WIDTH // seqs
    for h in range(2):
        for j in range(lead.shape[0] // 2):
            place = slice(j * ROW_TILE, (j + 1) * ROW_TILE)
            halves[0, h, :, place] = lead[h * (lead.shape[0] // 2) + j]
        halves[1, h] = tail[:, h * HALF : (h + 1) * HALF]
    states[seq] = codes[...].astype(jnp.float32).astype(jnp.bfloat16)
    logits[...] = jnp.zeros_like(logits)
    greet(groups, seqs)

    def part(c, g, h):
        in_lead = (lead_block == g).astype(jnp.float32)
        in_tail = (tail_block == g).astype(jnp.float32)
        here = slice(c * rows, (c + 1) * rows)
        value = halves[0, h, here] * in_lead + halves[1, h, here] * in_tail
        return value.astype(jnp.bfloat16)

    def half_to_mate(c, k):
        return send(
            stage.at[c, k], mate_in.at[c, k], halved.at[0, c, k], halved.at[1, c, k], tile=mate
        )

    def sum_to_owner(c, k):
        owner = ((group + k) % groups) * 2 + core
        return send(
            onward.at[c, k], arrived.at[c, k], summed.at[0, c, k], summed.at[1, c, k], tile=owner
        )

    def to_group(c, k):
        other = ((group + k) % groups) * 2 + core
        mine = every[c].at[group, core]
        return send(mine, mine, near.at[0, c, k], near.at[1, c, k], tile=other)

    def to_mate(c, k):
        block = every[c].at[(group + groups - k) % groups, core]
        return send(block, block, pair.at[0, c, k], pair.at[1, c, k], tile=mate)

    def tail_to(c, k):
        place = tails.at[seq, pl.ds(c * rows, rows)]
        return send(tail_out[c], place, over.at[0, c, k], over.at[1, c, k], seq=(seq + k) % seqs)

    def lead_to(c, k):
        other = (seq + k) % seqs
        place = leads.at[seq, pl.ds(c * rows, rows)]
        return send(
            lead_out.at[c, other], place, over.at[2, c, k], over.at[3, c, k], seq=other
        )

    def states_to(k):
        own = states.at[seq]
        return send(own, own, shared.at[0, k], shared.at[1, k], seq=(seq + k) % seqs)

    def each(low, high, act):
        def step(k, carry):
            act(k)
            return carry

        lax.fori_loop(low, high, step, 0)

    def halve(c):
        def act(k):
            k = (k + 1) % groups
            stage[c, k] = part(c, (group + k) % groups, 1 - core)
            half_to_mate(c, k).start()

        each(0, groups, act)

    def reduce_start(c):
        def act(k):
            own = part(c, (group + k) % groups, core).astype(jnp.float32)
            half_to_mate(c, k).wait_recv()
            onward[c, k] = (own + mate_in[c, k].astype(jnp.float32)).astype(jnp.bfloat16)
            sum_to_owner(c, k).start()

        each(1, groups, act)

    def reduce_end(c):
        half_to_mate(c, 0).wait_recv()
        own = part(c, group, core).astype(jnp.float32) + mate_in[c, 0].astype(jnp.float32)
        logits[:, :HALF] = own + fields[...]

        def act(k):
            sum_to_owner(c, k).wait_recv()
            logits[:, :HALF] += arrived[c, k].astype(jnp.float32)

        each(1, groups, act)
        result = normalize(logits[...])[:, :HALF].astype(jnp.bfloat16)
        every[c][group, core] = result
        each(1, groups, lambda k: to_group(c, k).start())
        to_mate(c, 0).start()
        probs[c * rows : (c + 1) * rows] = result

    def relay(c):
        def act(k):
            to_group(c, k).wait_recv()
            to_mate(c, k).start()

        each(1, groups, act)
        each(0, groups, lambda k: to_mate(c, k).wait_recv())
        for h in range(2):
            tail_out[c][:, h * HALF : (h + 1) * HALF] = every[c][tail_block, h]
            block_half = every[c][lead_block, h]
            for j in range(seqs // 2):
                lead_out[c, h * (seqs // 2) + j] = block_half[:, j * share : (j + 1) * share]

        def start(k):
            tail_to(c, k).start()
            lead_to(c, k).start()

        each(1, seqs, start)
        tails[seq, c * rows : (c + 1) * rows] = tail_out[c][...]
        leads[seq, c * rows : (c + 1) * rows] = lead_out[c, seq]

    def finish(c):
        def ends(k):
            tail_to(c, k).wait()
            lead_to(c, k).wait()

        each(1, seqs, ends)

        def sent(k):
            to_group(c, k).wait_send()
            sum_to_owner(c, k).wait_send()

        each(1, groups, sent)

        def passed(k):
            to_mate(c, k).wait_send()
            half_to_mate(c, k).wait_send()

        each(0, groups, passed)

    halve(0)
    halve(1)
    reduce_start(0)
    each(1, seqs, lambda k: states_to(k).start())
    reduce_start(1)
    for c in range(2, CHUNKS):
        halve(c)
    for c in range(CHUNKS + 1):
        if c < CHUNKS:
            reduce_end(c)
        if c + 2 < CHUNKS:
            reduce_start(c + 2)
        if c > 0:
            relay(c - 1)
    for c in range(CHUNKS):
        finish(c)
    each(1, seqs, lambda k: states_to(k).wait())


def exchange(tile_blocks, lead, tail, states, fields, groups, seqs):
    rows = tail.shape[0]
    part = rows // CHUNKS
    vmem = pl.BlockSpec(memory_space=pltpu.VMEM)
    slots = pltpu.VMEM((CHUNKS, groups, part, HALF), jnp.bfloat16)
    pair_sems = pltpu.SemaphoreType.DMA((2, CHUNKS, groups))
    return pl.pallas_call(
        functools.partial(exchange_kernel, groups, seqs),
        out_shape=[
            jax.ShapeDtypeStruct((rows, HALF), jnp.bfloat16),
            jax.ShapeDtypeStruct((seqs, rows, WIDTH), jnp.bfloat16),
            jax.ShapeDtypeStruct((seqs, rows, WIDTH // seqs), jnp.bfloat16),
            jax.ShapeDtypeStruct((seqs,) + states.shape, jnp.bfloat16),
        ],
        in_specs=[pl.BlockSpec(memory_space=pltpu.SMEM)] + [vmem] * 4,
        out_specs=[vmem] * 4,
        scratch_shapes=[pltpu.VMEM((groups, 2, part, HALF), jnp.bfloat16)] * CHUNKS
        + [pltpu.VMEM((part, WIDTH), jnp.bfloat16)] * CHUNKS
        + [
            pltpu.VMEM((CHUNKS, seqs, part, WIDTH // seqs), jnp.bfloat16),
            pltpu.VMEM((2, 2, rows, HALF), jnp.float32),
            pltpu.VMEM((part, 1024), jnp.float32),
            slots,
            slots,
            slots,
            slots,
            pair_sems,
            pair_sems,
            pair_sems,
            pair_sems,
            pltpu.SemaphoreType.DMA((4, CHUNKS, seqs)),
            pltpu.SemaphoreType.DMA((2, seqs)),
        ],
        compiler_params=pltpu.CompilerParams(
            collective_id=0, has_side_effects=True, vmem_limit_bytes=60 << 20
        ),
    )(tile_blocks, lead, tail, states, fields)


def body(states, tile_blocks, couplings, fields):
    groups = lax.axis_size("tile") // 2
    seqs = lax.axis_size("seq")
    row_total = states.shape[0] * seqs
    share = WIDTH // seqs
    lead, tail = tile_fields(tile_blocks, states, couplings)
    probs, tail_probs, lead_probs, all_states = exchange(
        tile_blocks, lead, tail, states, fields[None, :], groups, seqs
    )
    grad = gradient(
        tile_blocks,
        all_states.reshape(row_total, states.shape[1]),
        lead_probs.reshape(row_total, share),
        tail_probs.reshape(row_total, WIDTH),
    )
    return (probs, grad[None])


def solution(mesh):
    in_specs = (P("seq", None), P("tile", None), P("tile", None, None), P("tile"))
    out_specs = (P("seq", "tile"), P("tile", "seq", None))
    return jax.shard_map(body, mesh=mesh, in_specs=in_specs, out_specs=out_specs, check_vma=False)
```

```python
import functools
import math

import jax
import jax.numpy as jnp
from jax import lax
from jax.experimental import pallas as pl
from jax.experimental.pallas import tpu as pltpu
from jax.sharding import PartitionSpec as P

Q = 21
LB = 96
WIDTH = LB * Q
HALF = WIDTH // 2
CHUNKS = 4
ROW_TILE = WIDTH // 6
COLUMN_TILE = 512


def residue_of(index):
    return (index * 3121) >> 16


def table(states, first, columns):
    lanes = states.shape[1]
    residue = residue_of(lax.broadcasted_iota(jnp.int32, (lanes, columns), 1)) + first
    place = lax.broadcasted_iota(jnp.int32, (lanes, columns), 0) == residue
    spread = jnp.dot(
        states, place.astype(jnp.float32).astype(jnp.bfloat16), preferred_element_type=jnp.float32
    )
    column = lax.broadcasted_iota(jnp.int32, (1, columns), 1)
    code = (column - residue_of(column) * Q).astype(jnp.float32)
    return jnp.where(spread == code, 1.0, 0.0)


def normalize(logits):
    lanes = logits.shape[1]
    lane = lax.broadcasted_iota(jnp.int32, (1, lanes), 1)
    place = lane - residue_of(lane) * Q
    shifts = (1, 2, 4, 8, 16)
    top = logits
    for shift in shifts:
        top = jnp.where(place >= shift, jnp.maximum(top, pltpu.roll(top, shift, 1)), top)
    for shift in shifts:
        back = pltpu.roll(top, lanes - shift, 1)
        top = jnp.where(place + shift < Q, jnp.maximum(top, back), top)
    exponent = jnp.exp(logits - top)
    total = exponent
    for shift in shifts:
        total = total + jnp.where(place >= shift, pltpu.roll(total, shift, 1), 0.0)
    total = jnp.where(place == Q - 1, total, 0.0)
    for shift in shifts:
        back = pltpu.roll(total, lanes - shift, 1)
        total = jnp.where(place + shift < Q, jnp.maximum(total, back), total)
    return exponent / total


def field_kernel(blocks, codes, weights, lead, tail, tail_table, states):
    step = pl.program_id(0)
    rows, width = weights.shape[1], weights.shape[2]
    first = step * (rows // Q)

    @pl.when(step == 0)
    def _():
        states[...] = codes[...].astype(jnp.float32).astype(jnp.bfloat16)
        tail_table[...] = table(states[...], blocks[0, 1] * LB, width).astype(jnp.bfloat16)
        tail[...] = jnp.zeros_like(tail)

    own = residue_of(lax.broadcasted_iota(jnp.int32, (rows, 1), 0)) + first
    own = jnp.where(blocks[0, 0] == blocks[0, 1], own, -1)
    other = residue_of(lax.broadcasted_iota(jnp.int32, (1, width), 1))
    kept = jnp.where(own == other, 0.0, weights[0].astype(jnp.float32)).astype(jnp.bfloat16)
    lead_table = table(states[...], blocks[0, 0] * LB + first, rows).astype(jnp.bfloat16)
    lead[0] = lax.dot_general(
        tail_table[...], kept, (((1,), (1,)), ((), ())), preferred_element_type=jnp.float32
    )
    tail[...] += jnp.dot(lead_table, kept, preferred_element_type=jnp.float32)


def tile_fields(tile_blocks, states, couplings):
    rows = states.shape[0]
    return pl.pallas_call(
        field_kernel,
        grid=(WIDTH // ROW_TILE,),
        out_shape=[
            jax.ShapeDtypeStruct((WIDTH // ROW_TILE, rows, ROW_TILE), jnp.float32),
            jax.ShapeDtypeStruct((rows, WIDTH), jnp.float32),
        ],
        in_specs=[
            pl.BlockSpec(memory_space=pltpu.SMEM),
            pl.BlockSpec(states.shape, lambda i: (0, 0)),
            pl.BlockSpec((1, ROW_TILE, WIDTH), lambda i: (0, i, 0)),
        ],
        out_specs=[
            pl.BlockSpec((1, rows, ROW_TILE), lambda i: (i, 0, 0)),
            pl.BlockSpec((rows, WIDTH), lambda i: (0, 0)),
        ],
        scratch_shapes=[
            pltpu.VMEM((rows, WIDTH), jnp.bfloat16),
            pltpu.VMEM(states.shape, jnp.bfloat16),
        ],
        compiler_params=pltpu.CompilerParams(vmem_limit_bytes=60 << 20),
    )(tile_blocks, states, couplings)


def gradient_kernel(blocks, states, lead_probs, tail_probs, probs, grad, turned, left):
    step = pl.program_id(0)
    rows, share = lead_probs.shape
    columns = tail_probs.shape[1]
    first = lax.axis_index("seq") * (share // Q)
    lanes = states.shape[1]

    @pl.when(step == 0)
    def _():
        row = lax.broadcasted_iota(jnp.int32, (share, lanes), 0)
        lane = lax.broadcasted_iota(jnp.int32, (share, lanes), 1)
        here = residue_of(row) + first + blocks[0, 0] * LB
        place = (lane == here).astype(jnp.float32).astype(jnp.bfloat16)
        spread = lax.dot_general(
            place, states[...], (((1,), (1,)), ((), ())), preferred_element_type=jnp.float32
        )
        row = lax.broadcasted_iota(jnp.int32, (share, 1), 0)
        code = (row - residue_of(row) * Q).astype(jnp.float32)
        lead_table = jnp.where(spread == code, 1.0, 0.0)
        lead_gap = lead_probs[...].astype(jnp.float32).T - lead_table
        left[:, :rows] = lead_gap.astype(jnp.bfloat16)
        left[:, rows:] = lead_table.astype(jnp.bfloat16)
        turned[...] = probs[...].astype(jnp.float32).T.astype(jnp.bfloat16)

    start = step * columns
    residue = residue_of(lax.broadcasted_iota(jnp.int32, (lanes, columns), 1) + start)
    here = residue + blocks[0, 1] * LB
    place = lax.broadcasted_iota(jnp.int32, (lanes, columns), 0) == here
    spread = jnp.dot(
        states[...],
        place.astype(jnp.float32).astype(jnp.bfloat16),
        preferred_element_type=jnp.float32,
    )
    column = lax.broadcasted_iota(jnp.int32, (1, columns), 1) + start
    other = residue_of(column)
    code = (column - other * Q).astype(jnp.float32)
    tail_table = jnp.where(spread == code, 1.0, 0.0)
    tail_gap = (tail_probs[...].astype(jnp.float32) - tail_table).astype(jnp.bfloat16)
    total = jnp.dot(
        left[:, :rows], tail_table.astype(jnp.bfloat16), preferred_element_type=jnp.float32
    )
    total = total + jnp.dot(left[:, rows:], tail_gap, preferred_element_type=jnp.float32)
    own = residue_of(lax.broadcasted_iota(jnp.int32, (share, 1), 0)) + first
    own = jnp.where(blocks[0, 0] == blocks[0, 1], own, -1)
    grad[...] = jnp.where(own == other, 0.0, total * (Q / math.sqrt(rows)))


def gradient(tile_blocks, states, lead_probs, tail_probs, probs):
    rows, share = lead_probs.shape
    return pl.pallas_call(
        gradient_kernel,
        grid=(pl.cdiv(WIDTH, COLUMN_TILE),),
        out_shape=[
            jax.ShapeDtypeStruct((share, WIDTH), jnp.float32),
            jax.ShapeDtypeStruct(probs.shape[::-1], jnp.bfloat16),
        ],
        in_specs=[
            pl.BlockSpec(memory_space=pltpu.SMEM),
            pl.BlockSpec(states.shape, lambda i: (0, 0)),
            pl.BlockSpec((rows, share), lambda i: (0, 0)),
            pl.BlockSpec((rows, COLUMN_TILE), lambda i: (0, i)),
            pl.BlockSpec(probs.shape, lambda i: (0, 0)),
        ],
        out_specs=[
            pl.BlockSpec((share, COLUMN_TILE), lambda i: (0, i)),
            pl.BlockSpec(probs.shape[::-1], lambda i: (0, 0)),
        ],
        scratch_shapes=[pltpu.VMEM((share, 2 * rows), jnp.bfloat16)],
        compiler_params=pltpu.CompilerParams(vmem_limit_bytes=60 << 20),
    )(tile_blocks, states, lead_probs, tail_probs, probs)


def send(src, dst, send_sem, recv_sem, **device):
    return pltpu.make_async_remote_copy(
        src_ref=src,
        dst_ref=dst,
        send_sem=send_sem,
        recv_sem=recv_sem,
        device_id=device,
        device_id_type=pl.DeviceIdType.MESH,
    )


def greet(groups, seqs):
    tile = lax.axis_index("tile")
    group, core = tile // 2, tile % 2
    seq = lax.axis_index("seq")
    barrier = pltpu.get_barrier_semaphore()
    mesh_id = pl.DeviceIdType.MESH
    pl.semaphore_signal(
        barrier, inc=1, device_id={"tile": group * 2 + 1 - core}, device_id_type=mesh_id
    )
    for k in range(1, groups):
        pl.semaphore_signal(
            barrier,
            inc=1,
            device_id={"tile": ((group + k) % groups) * 2 + core},
            device_id_type=mesh_id,
        )
    for k in range(1, seqs):
        pl.semaphore_signal(
            barrier, inc=1, device_id={"seq": (seq + k) % seqs}, device_id_type=mesh_id
        )
    pl.semaphore_wait(barrier, groups + max(seqs - 1, 0))


def exchange_kernel(
    groups, seqs, blocks, lead, tail, codes, fields, probs, tails, leads, states, *scratch
):
    every = scratch[:CHUNKS]
    tail_out = scratch[CHUNKS : 2 * CHUNKS]
    (lead_out, halves, logits, stage, mate_in, onward, arrived) = scratch[2 * CHUNKS : -6]
    (halved, summed, near, pair, over, shared) = scratch[-6:]
    tile = lax.axis_index("tile")
    group, core = tile // 2, tile % 2
    seq = lax.axis_index("seq")
    mate = group * 2 + 1 - core
    lead_block, tail_block = blocks[0, 0], blocks[0, 1]
    rows = probs.shape[0] // CHUNKS
    share = WIDTH // seqs
    for h in range(2):
        for j in range(lead.shape[0] // 2):
            place = slice(j * ROW_TILE, (j + 1) * ROW_TILE)
            halves[0, h, :, place] = lead[h * (lead.shape[0] // 2) + j]
        halves[1, h] = tail[:, h * HALF : (h + 1) * HALF]
    states[seq] = codes[...].astype(jnp.float32).astype(jnp.bfloat16)
    logits[...] = jnp.zeros_like(logits)
    greet(groups, seqs)

    def part(c, g, h):
        in_lead = (lead_block == g).astype(jnp.float32)
        in_tail = (tail_block == g).astype(jnp.float32)
        here = slice(c * rows, (c + 1) * rows)
        value = halves[0, h, here] * in_lead + halves[1, h, here] * in_tail
        return value.astype(jnp.bfloat16)

    def half_to_mate(c, k):
        return send(
            stage.at[c, k], mate_in.at[c, k], halved.at[0, c, k], halved.at[1, c, k], tile=mate
        )

    def sum_to_owner(c, k):
        owner = ((group + k) % groups) * 2 + core
        return send(
            onward.at[c, k], arrived.at[c, k], summed.at[0, c, k], summed.at[1, c, k], tile=owner
        )

    def to_group(c, k):
        other = ((group + k) % groups) * 2 + core
        mine = every[c].at[group, core]
        return send(mine, mine, near.at[0, c, k], near.at[1, c, k], tile=other)

    def to_mate(c, k):
        block = every[c].at[(group + groups - k) % groups, core]
        return send(block, block, pair.at[0, c, k], pair.at[1, c, k], tile=mate)

    def tail_to(c, k):
        place = tails.at[seq, pl.ds(c * rows, rows)]
        return send(tail_out[c], place, over.at[0, c, k], over.at[1, c, k], seq=(seq + k) % seqs)

    def lead_to(c, k):
        other = (seq + k) % seqs
        place = leads.at[seq, pl.ds(c * rows, rows)]
        return send(
            lead_out.at[c, other], place, over.at[2, c, k], over.at[3, c, k], seq=other
        )

    def states_to(k):
        own = states.at[seq]
        return send(own, own, shared.at[0, k], shared.at[1, k], seq=(seq + k) % seqs)

    def each(low, high, act):
        def step(k, carry):
            act(k)
            return carry

        lax.fori_loop(low, high, step, 0)

    def halve(c):
        def act(k):
            k = (k + 1) % groups
            stage[c, k] = part(c, (group + k) % groups, 1 - core)
            half_to_mate(c, k).start()

        each(0, groups, act)

    def reduce_start(c):
        def act(k):
            own = part(c, (group + k) % groups, core).astype(jnp.float32)
            half_to_mate(c, k).wait_recv()
            onward[c, k] = (own + mate_in[c, k].astype(jnp.float32)).astype(jnp.bfloat16)
            sum_to_owner(c, k).start()

        each(1, groups, act)

    def reduce_end(c):
        half_to_mate(c, 0).wait_recv()
        own = part(c, group, core).astype(jnp.float32) + mate_in[c, 0].astype(jnp.float32)
        logits[:, :HALF] = own + fields[...]

        def act(k):
            sum_to_owner(c, k).wait_recv()
            logits[:, :HALF] += arrived[c, k].astype(jnp.float32)

        each(1, groups, act)
        result = normalize(logits[...])[:, :HALF].astype(jnp.bfloat16)
        every[c][group, core] = result
        each(1, groups, lambda k: to_group(c, k).start())
        to_mate(c, 0).start()
        probs[c * rows : (c + 1) * rows] = result

    def relay(c):
        def act(k):
            to_group(c, k).wait_recv()
            to_mate(c, k).start()

        each(1, groups, act)
        each(0, groups, lambda k: to_mate(c, k).wait_recv())
        for h in range(2):
            tail_out[c][:, h * HALF : (h + 1) * HALF] = every[c][tail_block, h]
            block_half = every[c][lead_block, h]
            for j in range(seqs // 2):
                lead_out[c, h * (seqs // 2) + j] = block_half[:, j * share : (j + 1) * share]

        def start(k):
            tail_to(c, k).start()
            lead_to(c, k).start()

        each(1, seqs, start)
        tails[seq, c * rows : (c + 1) * rows] = tail_out[c][...]
        leads[seq, c * rows : (c + 1) * rows] = lead_out[c, seq]

    def finish(c):
        def ends(k):
            tail_to(c, k).wait()
            lead_to(c, k).wait()

        each(1, seqs, ends)

        def sent(k):
            to_group(c, k).wait_send()
            sum_to_owner(c, k).wait_send()

        each(1, groups, sent)

        def passed(k):
            to_mate(c, k).wait_send()
            half_to_mate(c, k).wait_send()

        each(0, groups, passed)

    halve(0)
    halve(1)
    reduce_start(0)
    each(1, seqs, lambda k: states_to(k).start())
    reduce_start(1)
    for c in range(2, CHUNKS):
        halve(c)
    for c in range(CHUNKS + 1):
        if c < CHUNKS:
            reduce_end(c)
        if c + 2 < CHUNKS:
            reduce_start(c + 2)
        if c > 0:
            relay(c - 1)
    for c in range(CHUNKS):
        finish(c)
    each(1, seqs, lambda k: states_to(k).wait())


def exchange(tile_blocks, lead, tail, states, fields, groups, seqs):
    rows = tail.shape[0]
    part = rows // CHUNKS
    vmem = pl.BlockSpec(memory_space=pltpu.VMEM)
    slots = pltpu.VMEM((CHUNKS, groups, part, HALF), jnp.bfloat16)
    pair_sems = pltpu.SemaphoreType.DMA((2, CHUNKS, groups))
    return pl.pallas_call(
        functools.partial(exchange_kernel, groups, seqs),
        out_shape=[
            jax.ShapeDtypeStruct((rows, HALF), jnp.bfloat16),
            jax.ShapeDtypeStruct((seqs, rows, WIDTH), jnp.bfloat16),
            jax.ShapeDtypeStruct((seqs, rows, WIDTH // seqs), jnp.bfloat16),
            jax.ShapeDtypeStruct((seqs,) + states.shape, jnp.bfloat16),
        ],
        in_specs=[pl.BlockSpec(memory_space=pltpu.SMEM)] + [vmem] * 4,
        out_specs=[vmem] * 4,
        scratch_shapes=[pltpu.VMEM((groups, 2, part, HALF), jnp.bfloat16)] * CHUNKS
        + [pltpu.VMEM((part, WIDTH), jnp.bfloat16)] * CHUNKS
        + [
            pltpu.VMEM((CHUNKS, seqs, part, WIDTH // seqs), jnp.bfloat16),
            pltpu.VMEM((2, 2, rows, HALF), jnp.float32),
            pltpu.VMEM((part, 1024), jnp.float32),
            slots,
            slots,
            slots,
            slots,
            pair_sems,
            pair_sems,
            pair_sems,
            pair_sems,
            pltpu.SemaphoreType.DMA((4, CHUNKS, seqs)),
            pltpu.SemaphoreType.DMA((2, seqs)),
        ],
        compiler_params=pltpu.CompilerParams(
            collective_id=0, has_side_effects=True, vmem_limit_bytes=60 << 20
        ),
    )(tile_blocks, lead, tail, states, fields)


def body(states, tile_blocks, couplings, fields):
    groups = lax.axis_size("tile") // 2
    seqs = lax.axis_size("seq")
    row_total = states.shape[0] * seqs
    share = WIDTH // seqs
    lead, tail = tile_fields(tile_blocks, states, couplings)
    probs, tail_probs, lead_probs, all_states = exchange(
        tile_blocks, lead, tail, states, fields[None, :], groups, seqs
    )
    grad, turned = gradient(
        tile_blocks,
        all_states.reshape(row_total, states.shape[1]),
        lead_probs.reshape(row_total, share),
        tail_probs.reshape(row_total, WIDTH),
        probs,
    )
    return (turned.T, grad[None])


def solution(mesh):
    in_specs = (P("seq", None), P("tile", None), P("tile", None, None), P("tile"))
    out_specs = (P("seq", "tile"), P("tile", "seq", None))
    return jax.shard_map(body, mesh=mesh, in_specs=in_specs, out_specs=out_specs, check_vma=False)
```
